128 devices in a mesh: cuts: 16 (over x_hi, z, core), fsdp: 8 (over y, x_lo).
Axes of the slice: x: 4 (x_hi: 2, x_lo: 2; x = x_hi * 2 + x_lo), y: 4, z: 4, core: 2. Of those that a mesh axis runs over, the one named last changes fastest.
Arguments:
- outer: float32 [16, 1024, 4096], P('cuts', 'fsdp'), may hold values from -6 to 6
- inner: float32 [16, 1024, 4096], P('cuts', 'fsdp'), may hold values from -6 to 6
- momentum: float32 [16, 1024, 4096], P('cuts', 'fsdp'), may hold values from -3 to 3
- partner: int32 [16], replicated, may hold values from 0 to 15, as said below
Outputs:
- new_outer: float32 [16, 1024, 4096], P('cuts', 'fsdp')
- new_momentum: float32 [16, 1024, 4096], P('cuts', 'fsdp')
- weights: bfloat16 [16, 1024, 4096], P('cuts')
The draws below stay inside these ranges and needn't reach their ends.
Inputs may be any that keep to these rules, and one draw needn't show every extreme that they name: partner is a perfect matching of the 16 replicas: partner[partner[r]] = r and partner[r] != r.
All inputs are finite; a program needn't handle non-finite values.
Results may differ from the reference program's by a relative error of at most 0.001.
Values may be sent and summed in bfloat16 or wider, within the bound.
A program may use at most 128 MiB of HBM per device.

```python
import jax
import jax.numpy as jnp

D = 4096
ROWS = 1024
REPLICAS = 16


def draw_partner(key, part):
    key = jax.random.fold_in(key, 7)
    order = jax.random.permutation(key, REPLICAS).astype(jnp.int32)
    firsts = order[0::2]
    seconds = order[1::2]
    paired = jnp.zeros((REPLICAS,), dtype=jnp.int32)
    paired = paired.at[firsts].set(seconds)
    paired = paired.at[seconds].set(firsts)
    return paired


def block_scale(own_key, shape, cuts, least, top_value):
    gain, own = 1.0, jax.random.fold_in(own_key, 6)
    for dim, blocks in cuts:
        draws = jnp.exp(jax.random.uniform(jax.random.fold_in(own, dim), (blocks,), jnp.float32, least / len(cuts), top_value / len(cuts)))
        gain = gain * jnp.repeat(draws, shape[dim] // blocks).reshape([-1 if axis == dim else 1 for axis in range(len(shape))])
    return gain


def normal_values(rng, dims, scale, reach, split=(), kind=jnp.bfloat16):
    array = jax.random.normal(rng, dims, jnp.float32) * scale
    if len(split) > 0:
        array = block_scale(rng, dims, split, -0.22, 0.18) * array
    return jnp.clip(array, min=-reach, max=reach).astype(kind)


def setup_inputs(seed: int = 0) -> dict:
    seeds = jax.random.split(jax.random.key(seed), 5)
    outer = normal_values(seeds[0], (REPLICAS, ROWS, D), 1.0, 6.0, ((0, 16), (1, 8)), jnp.float32)
    inner = normal_values(seeds[1], (REPLICAS, ROWS, D), 1.0, 6.0, ((0, 16), (1, 8)), jnp.float32)
    momentum = normal_values(seeds[2], (REPLICAS, ROWS, D), 0.5, 3.0, ((0, 16), (1, 8)), jnp.float32)
    partner = draw_partner(jax.random.fold_in(seeds[4], 71), 0)
    return dict(outer=outer, inner=inner, momentum=momentum, partner=partner)


momentum_decay = 0.6
outer_rate = 0.7
pull_weight = 0.5


def reference(outer, inner, momentum, partner):
    delta = outer - inner
    mate_delta = jnp.take(delta, partner, axis=0)
    mate_momentum = jnp.take(momentum, partner, axis=0)
    mate_outer = jnp.take(outer, partner, axis=0)
    drift = (delta + mate_delta) * 0.5 + pull_weight * (outer - mate_outer) * 0.5
    new_momentum = momentum_decay * (momentum + mate_momentum) * 0.5 + drift
    new_outer = outer - outer_rate * (drift + momentum_decay * new_momentum)
    return new_outer, new_momentum, new_outer.astype(jnp.bfloat16)
```

```python
import functools

import jax
import jax.numpy as jnp
from jax import lax
from jax.experimental import pallas as pl
from jax.experimental.pallas import tpu as pltpu
from jax.sharding import PartitionSpec as P

momentum_decay = 0.6
outer_rate = 0.7
pull_weight = 0.5

MESH = pl.DeviceIdType.MESH
STEPS = 32767.0
GROUP = 8
SLICES = 4
LANES = 128


def terms(outer, inner, momentum):
    pull = (0.5 - 0.5 * pull_weight) * outer - 0.5 * inner
    half = 0.5 * momentum_decay * momentum
    return pull + half, (1.0 + momentum_decay) * pull + momentum_decay * half


def kernel(
    chunks, outer, inner, momentum, partner, new_outer, new_momentum, weights,
    o_v, i_v, m_v, w_v, packed, mixed, stage, picked, final, inverse, scale, scale_mixed, scale_picked, scale_final,
    load_sem, store_sem, scale_send, scale_recv, out1_send, out1_recv, half_send, half_recv, out2_send, out2_recv,
    gather_send, gather_recv,
):
    rows = o_v.shape[0] // chunks
    c, f = lax.axis_index("cuts"), lax.axis_index("fsdp")
    half, place = c // GROUP, c % GROUP
    base = half * GROUP
    y, xl = f // 2, f % 2

    def mate(k):
        return base + (place + k) % GROUP, f

    across = ((1 - half) * GROUP + place, f)
    beside = (c, y * 2 + 1 - xl)
    up = (c, ((y + 1) % 4) * 2 + xl)
    down = (c, ((y + 3) % 4) * 2 + xl)
    peers = [mate(k) for k in range(1, GROUP)] + [across, beside, up, down]

    loads = [
        pltpu.make_async_copy(src.at[0], dst, load_sem.at[k])
        for k, (src, dst) in enumerate(((outer, o_v), (inner, i_v), (momentum, m_v)))
    ]
    for copy in loads:
        copy.start()
    barrier = pltpu.get_barrier_semaphore()
    for peer in peers:
        pl.semaphore_signal(barrier, inc=1, device_id=peer, device_id_type=MESH)
    for copy in loads:
        copy.wait()

    def measure_scale(j, carry):
        for s in range(SLICES):
            cols = pl.ds(pl.multiple_of((j * SLICES + s) * LANES, LANES), LANES)
            first, second = terms(o_v[:, cols], i_v[:, cols], m_v[:, cols])
            for row, term in ((s, first), (SLICES + s, second)):
                top = jnp.max(jnp.abs(term), axis=0, keepdims=True)
                scale[j, row : row + 1, :] = top * (1.0 / STEPS)
                inverse[j, row : row + 1, :] = jnp.where(top > 1e-30, STEPS / jnp.maximum(top, 1e-30), 0.0)
        return carry

    lax.fori_loop(0, GROUP, measure_scale, 0)

    def pack(i):
        here = pl.ds(pl.multiple_of(i * rows, rows), rows)

        def one(j, carry):
            for s in range(SLICES):
                cols = pl.ds(pl.multiple_of((j * SLICES + s) * LANES, LANES), LANES)
                first, second = terms(o_v[here, cols], i_v[here, cols], m_v[here, cols])
                a = jnp.round(first * inverse[j, s : s + 1, :]).astype(jnp.int32)
                b = jnp.round(second * inverse[j, SLICES + s : SLICES + s + 1, :]).astype(jnp.int32)
                packed[i, j, s * rows : (s + 1) * rows, :] = (a << 16) | (b & 0xFFFF)
            return carry

        lax.fori_loop(0, GROUP, one, 0)

    def spread(source, target, slot, send, recv):
        keep = pltpu.make_async_copy(source.at[place], target.at[slot], recv)
        keep.start()
        for k in range(1, GROUP):
            j = (place + k) % GROUP
            pltpu.make_async_remote_copy(
                src_ref=source.at[j], dst_ref=target.at[slot], send_sem=send, recv_sem=recv,
                device_id=mate(k), device_id_type=MESH,
            ).start()

    def wait(ref, sem):
        pltpu.make_async_copy(ref, ref, sem).wait()

    def send_out(i):
        pack(i)
        spread(packed.at[i], mixed.at[i], c, out1_send.at[i], out1_recv.at[i])

    def swap_halves(i):
        mine = mixed.at[i, pl.ds(base, GROUP)]
        wait(mine, out1_recv.at[i])
        pltpu.make_async_remote_copy(
            src_ref=mine, dst_ref=mine, send_sem=half_send.at[i], recv_sem=half_recv.at[i],
            device_id=across, device_id_type=MESH,
        ).start()

    def send_back(i):
        wait(mixed.at[i, pl.ds((1 - half) * GROUP, GROUP)], half_recv.at[i])
        stage[...] = mixed[i]
        for k in range(GROUP):
            picked[i, k] = stage[partner[base + k]]
        spread(picked.at[i], final.at[i], place, out2_send.at[i], out2_recv.at[i])

    def block(device, i):
        return weights.at[0, pl.ds(pl.multiple_of(device * (rows * chunks) + i * rows, rows), rows)]

    def hand(i, source, owner, target, slot):
        pltpu.make_async_remote_copy(
            src_ref=source, dst_ref=block(owner, i), send_sem=gather_send.at[i, slot], recv_sem=gather_recv.at[i, slot],
            device_id=target, device_id_type=MESH,
        ).start()

    def update(i):
        here = pl.ds(pl.multiple_of(i * rows, rows), rows)
        wait(final.at[i], out2_recv.at[i])

        def one(j, carry):
            for s in range(SLICES):
                cols = pl.ds(pl.multiple_of((j * SLICES + s) * LANES, LANES), LANES)
                word = final[i, j, s * rows : (s + 1) * rows, :]
                first = (word >> 16).astype(jnp.float32) * scale_final[j, s : s + 1, :]
                second = ((word << 16) >> 16).astype(jnp.float32) * scale_final[j, SLICES + s : SLICES + s + 1, :]
                own, old = o_v[here, cols], m_v[here, cols]
                push = (0.5 + 0.5 * pull_weight) * own - 0.5 * i_v[here, cols]
                momentum_part = (0.5 * momentum_decay) * old
                m_v[here, cols] = momentum_part + push + first
                step = (1.0 + momentum_decay) * push + momentum_decay * momentum_part + second
                result = own - outer_rate * step
                o_v[here, cols] = result
                w_v[here, cols] = result.astype(jnp.bfloat16)
            return carry

        lax.fori_loop(0, GROUP, one, 0)
        own = w_v.at[here]
        hand(i, own, f, beside, 0)
        hand(i, own, f, up, 1)
        hand(i, own, f, down, 3)
        pltpu.make_async_copy(own, block(f, i), store_sem.at[i, 0]).start()
        pltpu.make_async_copy(o_v.at[here], new_outer.at[0, here], store_sem.at[i, 1]).start()
        pltpu.make_async_copy(m_v.at[here], new_momentum.at[0, here], store_sem.at[i, 2]).start()

    def arrived(i, slot):
        wait(w_v.at[pl.ds(0, rows)], gather_recv.at[i, slot])

    def pass_neighbour(i):
        other = y * 2 + 1 - xl
        arrived(i, 0)
        hand(i, block(other, i), other, up, 2)
        hand(i, block(other, i), other, down, 4)

    def pass_far(i):
        below, above = ((y + 3) % 4) * 2, ((y + 1) % 4) * 2

        @pl.when(i % 2 == 0)
        def _():
            arrived(i, 1)
            hand(i, block(below + xl, i), below + xl, up, 5)
            arrived(i, 2)
            hand(i, block(below + 1 - xl, i), below + 1 - xl, up, 6)

        @pl.when(i % 2 == 1)
        def _():
            arrived(i, 3)
            hand(i, block(above + xl, i), above + xl, down, 5)
            arrived(i, 4)
            hand(i, block(above + 1 - xl, i), above + 1 - xl, down, 6)

    pack(0)
    pl.semaphore_wait(barrier, len(peers))
    spread(scale, scale_mixed, c, scale_send.at[0], scale_recv.at[0])
    spread(packed.at[0], mixed.at[0], c, out1_send.at[0], out1_recv.at[0])

    own_scales = scale_mixed.at[pl.ds(base, GROUP)]
    wait(own_scales, scale_recv.at[0])
    swap_scales = pltpu.make_async_remote_copy(
        src_ref=own_scales, dst_ref=own_scales, send_sem=scale_send.at[1], recv_sem=scale_recv.at[1],
        device_id=across, device_id_type=MESH,
    )
    swap_scales.start()

    def turn(t, carry):
        for stage_of, lag in (
            (send_out, -1), (swap_halves, 0), (send_back, 1), (update, 2), (pass_neighbour, 3), (pass_far, 4)
        ):
            @pl.when((t - lag >= 0) & (t - lag < chunks))
            def _(stage_of=stage_of, lag=lag):
                if stage_of is send_back:
                    @pl.when(t == lag)
                    def _():
                        wait(scale_mixed.at[pl.ds((1 - half) * GROUP, GROUP)], scale_recv.at[1])
                        for k in range(GROUP):
                            scale_picked[k] = scale_mixed[partner[base + k]]
                        spread(scale_picked, scale_final, place, scale_send.at[2], scale_recv.at[2])
                if stage_of is update:
                    @pl.when(t == lag)
                    def _():
                        wait(scale_final, scale_recv.at[2])
                stage_of(t - lag)
        return carry

    lax.fori_loop(0, chunks + 4, turn, 0)

    def drain(i, carry):
        @pl.when(i % 2 == 0)
        def _():
            arrived(i, 3)
            arrived(i, 4)

        @pl.when(i % 2 == 1)
        def _():
            arrived(i, 1)
            arrived(i, 2)

        arrived(i, 5)
        arrived(i, 6)
        for slot in range(7):
            wait(w_v.at[pl.ds(0, rows)], gather_send.at[i, slot])
        seven = pl.ds(0, GROUP - 1)
        wait(packed.at[i, seven], out1_send.at[i])
        wait(mixed.at[i, pl.ds(0, GROUP)], half_send.at[i])
        wait(picked.at[i, seven], out2_send.at[i])
        here = pl.ds(pl.multiple_of(i * rows, rows), rows)
        wait(w_v.at[here], store_sem.at[i, 0])
        wait(o_v.at[here], store_sem.at[i, 1])
        wait(m_v.at[here], store_sem.at[i, 2])
        return carry

    lax.fori_loop(0, chunks, drain, 0)
    seven = pl.ds(0, GROUP - 1)
    wait(scale.at[seven], scale_send.at[0])
    wait(own_scales, scale_send.at[1])
    wait(scale_picked.at[seven], scale_send.at[2])


def local(outer, inner, momentum, partner):
    _, rows, width = outer.shape
    chunks = 8
    high = rows // chunks * SLICES
    anywhere = pl.BlockSpec(memory_space=pl.ANY)
    wire = lambda *lead: pltpu.VMEM(lead + (high, LANES), jnp.int32)
    scales = lambda n: pltpu.VMEM((n, 2 * SLICES, LANES), jnp.float32)
    sems = lambda *shape: pltpu.SemaphoreType.DMA(shape)
    full = pltpu.VMEM((rows, width), jnp.float32)
    return pl.pallas_call(
        functools.partial(kernel, chunks),
        out_shape=(
            jax.ShapeDtypeStruct(outer.shape, jnp.float32),
            jax.ShapeDtypeStruct(outer.shape, jnp.float32),
            jax.ShapeDtypeStruct((1, rows * lax.axis_size("fsdp"), width), jnp.bfloat16),
        ),
        in_specs=[anywhere, anywhere, anywhere, pl.BlockSpec(memory_space=pltpu.SMEM)],
        out_specs=(anywhere, anywhere, anywhere),
        scratch_shapes=[
            full, full, full, pltpu.VMEM((rows, width), jnp.bfloat16),
            wire(chunks, GROUP), wire(chunks, 2 * GROUP), wire(2 * GROUP), wire(chunks, GROUP), wire(chunks, GROUP),
            scales(GROUP), scales(GROUP), scales(2 * GROUP), scales(GROUP), scales(GROUP),
            sems(3), sems(chunks, 3), sems(3), sems(3),
            sems(chunks), sems(chunks), sems(chunks), sems(chunks), sems(chunks), sems(chunks),
            sems(chunks, 7), sems(chunks, 7),
        ],
        compiler_params=pltpu.CompilerParams(
            collective_id=0, has_side_effects=True, vmem_limit_bytes=60 * 2**20
        ),
        name="outer_step",
    )(outer, inner, momentum, partner)


def solution(mesh):
    return jax.shard_map(
        local,
        mesh=mesh,
        in_specs=(P("cuts", "fsdp", None), P("cuts", "fsdp", None), P("cuts", "fsdp", None), P()),
        out_specs=(P("cuts", "fsdp", None), P("cuts", "fsdp", None), P("cuts", None, None)),
        check_vma=False,
    )
```

```python
import functools

import jax
import jax.numpy as jnp
from jax import lax
from jax.experimental import pallas as pl
from jax.experimental.pallas import tpu as pltpu
from jax.sharding import PartitionSpec as P

momentum_decay = 0.6
outer_rate = 0.7
pull_weight = 0.5

MESH = pl.DeviceIdType.MESH
STEPS = 32767.0
GROUP = 8
LANES = 128
HEIGHT = 16
PARTS = 2
LAGS = (-1, 0, 1, 2, 3, 4)


def terms(outer, inner, momentum):
    pull = (0.5 - 0.5 * pull_weight) * outer - 0.5 * inner
    half = 0.5 * momentum_decay * momentum
    return pull + half, (1.0 + momentum_decay) * pull + momentum_decay * half


def kernel(
    units, slices, outer, inner, momentum, partner, new_outer, new_momentum, weights,
    o_v, i_v, m_v, packed, mixed, stage, picked, final, inverse, scale, scale_mixed, scale_picked, scale_final,
    load_sem, scale_send, scale_recv, out1_send, out1_recv, half_send, half_recv, out2_send, out2_recv,
    gather_send, gather_recv,
):
    rows, width = o_v.shape
    levels, span = rows // HEIGHT, width // PARTS
    c, f = lax.axis_index("cuts"), lax.axis_index("fsdp")
    half, place = c // GROUP, c % GROUP
    base = half * GROUP
    y, xl = f // 2, f % 2

    def mate(k):
        return base + (place + k) % GROUP, f

    across = ((1 - half) * GROUP + place, f)
    beside = (c, y * 2 + 1 - xl)
    up = (c, ((y + 1) % 4) * 2 + xl)
    down = (c, ((y + 3) % 4) * 2 + xl)
    peers = [mate(k) for k in range(1, GROUP)] + [across, beside, up, down]

    barrier = pltpu.get_barrier_semaphore()
    for peer in peers:
        pl.semaphore_signal(barrier, inc=1, device_id=peer, device_id_type=MESH)
    loads = [
        [
            pltpu.make_async_copy(
                src.at[0, :, pl.ds(p * span, span)], dst.at[:, pl.ds(p * span, span)], load_sem.at[k, p]
            )
            for k, (src, dst) in enumerate(((outer, o_v), (inner, i_v), (momentum, m_v)))
        ]
        for p in range(PARTS)
    ]
    for part in loads:
        for copy in part:
            copy.start()

    def tile(p, j, q):
        return pl.ds(pl.multiple_of(p * span + (j * slices + q) * LANES, LANES), LANES)

    for p in range(PARTS):
        for copy in loads[p]:
            copy.wait()

        def measure_scale(j, carry, p=p):
            for q in range(slices):
                cols = tile(p, j, q)
                first, second = terms(o_v[:, cols], i_v[:, cols], m_v[:, cols])
                at = p * slices + q
                for row, term in ((at, first), (PARTS * slices + at, second)):
                    top = jnp.max(jnp.abs(term), axis=0, keepdims=True)
                    scale[j, row : row + 1, :] = top * (1.0 / STEPS)
                    inverse[j, row : row + 1, :] = jnp.where(top > 1e-30, STEPS / jnp.maximum(top, 1e-30), 0.0)
            return carry

        lax.fori_loop(0, GROUP, measure_scale, 0)

    def where(u):
        return u // levels, pl.ds(pl.multiple_of((u % levels) * HEIGHT, HEIGHT), HEIGHT)

    def pack(u):
        p, here = where(u)

        def one(j, carry):
            for q in range(slices):
                cols = tile(p, j, q)
                first, second = terms(o_v[here, cols], i_v[here, cols], m_v[here, cols])
                at = p * slices + q
                a = jnp.round(first * inverse[j, pl.ds(at, 1), :]).astype(jnp.int32)
                b = jnp.round(second * inverse[j, pl.ds(PARTS * slices + at, 1), :]).astype(jnp.int32)
                packed[u, j, q * HEIGHT : (q + 1) * HEIGHT, :] = (a << 16) | (b & 0xFFFF)
            return carry

        lax.fori_loop(0, GROUP, one, 0)

    def spread(source, target, slot, send, recv):
        keep = pltpu.make_async_copy(source.at[place], target.at[slot], recv)
        keep.start()
        for k in range(1, GROUP):
            j = (place + k) % GROUP
            pltpu.make_async_remote_copy(
                src_ref=source.at[j], dst_ref=target.at[slot], send_sem=send, recv_sem=recv,
                device_id=mate(k), device_id_type=MESH,
            ).start()

    def wait(ref, sem):
        pltpu.make_async_copy(ref, ref, sem).wait()

    def send_out(u):
        pack(u)
        spread(packed.at[u], mixed.at[u], c, out1_send.at[u], out1_recv.at[u])

    def swap_halves(u):
        mine = mixed.at[u, pl.ds(base, GROUP)]
        wait(mine, out1_recv.at[u])
        pltpu.make_async_remote_copy(
            src_ref=mine, dst_ref=mine, send_sem=half_send.at[u], recv_sem=half_recv.at[u],
            device_id=across, device_id_type=MESH,
        ).start()

    def send_back(u):
        wait(mixed.at[u, pl.ds((1 - half) * GROUP, GROUP)], half_recv.at[u])
        stage[...] = mixed[u]
        for k in range(GROUP):
            picked[u, k] = stage[partner[base + k]]
        spread(picked.at[u], final.at[u], place, out2_send.at[u], out2_recv.at[u])

    def block(device, u):
        p, _ = where(u)
        start = pl.multiple_of(device * rows + (u % levels) * HEIGHT, HEIGHT)
        return weights.at[0, pl.ds(start, HEIGHT), pl.ds(pl.multiple_of(p * span, span), span)]

    def hand(u, owner, target, slot):
        pltpu.make_async_remote_copy(
            src_ref=block(owner, u), dst_ref=block(owner, u),
            send_sem=gather_send.at[u, slot], recv_sem=gather_recv.at[u, slot],
            device_id=target, device_id_type=MESH,
        ).start()

    def update(u):
        p, here = where(u)
        wait(final.at[u], out2_recv.at[u])
        there = pl.ds(pl.multiple_of(f * rows + (u % levels) * HEIGHT, HEIGHT), HEIGHT)

        def one(j, carry):
            for q in range(slices):
                cols = tile(p, j, q)
                at = p * slices + q
                word = final[u, j, q * HEIGHT : (q + 1) * HEIGHT, :]
                first = (word >> 16).astype(jnp.float32) * scale_final[j, pl.ds(at, 1), :]
                second = ((word << 16) >> 16).astype(jnp.float32) * scale_final[j, pl.ds(PARTS * slices + at, 1), :]
                own = o_v[here, cols]
                push = (0.5 + 0.5 * pull_weight) * own - 0.5 * i_v[here, cols]
                momentum_part = (0.5 * momentum_decay) * m_v[here, cols]
                new_momentum[0, here, cols] = momentum_part + push + first
                step = (1.0 + momentum_decay) * push + momentum_decay * momentum_part + second
                result = own - outer_rate * step
                new_outer[0, here, cols] = result
                weights[0, there, cols] = result.astype(jnp.bfloat16)
            return carry

        lax.fori_loop(0, GROUP, one, 0)
        hand(u, f, beside, 0)
        hand(u, f, up, 1)
        hand(u, f, down, 3)

    def arrived(u, slot):
        wait(block(f, u), gather_recv.at[u, slot])

    def pass_neighbour(u):
        other = y * 2 + 1 - xl
        arrived(u, 0)
        hand(u, other, up, 2)
        hand(u, other, down, 4)

    def pass_far(u):
        below, above = ((y + 3) % 4) * 2, ((y + 1) % 4) * 2

        @pl.when(u % 2 == 0)
        def _():
            arrived(u, 1)
            hand(u, below + xl, up, 5)
            arrived(u, 2)
            hand(u, below + 1 - xl, up, 6)

        @pl.when(u % 2 == 1)
        def _():
            arrived(u, 3)
            hand(u, above + xl, down, 5)
            arrived(u, 4)
            hand(u, above + 1 - xl, down, 6)

    pack(0)
    pl.semaphore_wait(barrier, len(peers))
    spread(scale, scale_mixed, c, scale_send.at[0], scale_recv.at[0])
    spread(packed.at[0], mixed.at[0], c, out1_send.at[0], out1_recv.at[0])

    own_scales = scale_mixed.at[pl.ds(base, GROUP)]
    wait(own_scales, scale_recv.at[0])
    swap_scales = pltpu.make_async_remote_copy(
        src_ref=own_scales, dst_ref=own_scales, send_sem=scale_send.at[1], recv_sem=scale_recv.at[1],
        device_id=across, device_id_type=MESH,
    )
    swap_scales.start()

    def turn(t, carry):
        for stage_of, lag in zip((send_out, swap_halves, send_back, update, pass_neighbour, pass_far), LAGS):
            @pl.when((t - lag >= (1 if stage_of is send_out else 0)) & (t - lag < units))
            def _(stage_of=stage_of, lag=lag):
                if stage_of is send_back:
                    @pl.when(t == lag)
                    def _():
                        wait(scale_mixed.at[pl.ds((1 - half) * GROUP, GROUP)], scale_recv.at[1])
                        for k in range(GROUP):
                            scale_picked[k] = scale_mixed[partner[base + k]]
                        spread(scale_picked, scale_final, place, scale_send.at[2], scale_recv.at[2])
                if stage_of is update:
                    @pl.when(t == lag)
                    def _():
                        wait(scale_final, scale_recv.at[2])
                stage_of(t - lag)
        return carry

    lax.fori_loop(LAGS[0] + 1, units + LAGS[-1], turn, 0)

    def drain(u, carry):
        @pl.when(u % 2 == 0)
        def _():
            arrived(u, 3)
            arrived(u, 4)

        @pl.when(u % 2 == 1)
        def _():
            arrived(u, 1)
            arrived(u, 2)

        arrived(u, 5)
        arrived(u, 6)
        for slot in range(7):
            wait(block(f, u), gather_send.at[u, slot])
        seven = pl.ds(0, GROUP - 1)
        wait(packed.at[u, seven], out1_send.at[u])
        wait(mixed.at[u, pl.ds(0, GROUP)], half_send.at[u])
        wait(picked.at[u, seven], out2_send.at[u])
        return carry

    lax.fori_loop(0, units, drain, 0)
    seven = pl.ds(0, GROUP - 1)
    wait(scale.at[seven], scale_send.at[0])
    wait(own_scales, scale_send.at[1])
    wait(scale_picked.at[seven], scale_send.at[2])


def flush(*refs):
    count = len(refs) // 2
    copies = [pltpu.make_async_copy(refs[k], refs[count + k], refs[-1].at[k]) for k in range(count)]
    for copy in copies:
        copy.start()
    for copy in copies:
        copy.wait()


def local(outer, inner, momentum, partner):
    _, rows, width = outer.shape
    units = rows // HEIGHT * PARTS
    slices = width // (PARTS * GROUP * LANES)
    anywhere = pl.BlockSpec(memory_space=pl.ANY)
    wire = lambda *lead: pltpu.VMEM(lead + (slices * HEIGHT, LANES), jnp.int32)
    scales = lambda n: pltpu.VMEM((n, 2 * PARTS * slices, LANES), jnp.float32)
    sems = lambda *shape: pltpu.SemaphoreType.DMA(shape)
    full = pltpu.VMEM((rows, width), jnp.float32)
    hbm = lambda x: pltpu.with_memory_space_constraint(x, pltpu.HBM)
    results = pl.pallas_call(
        functools.partial(kernel, units, slices),
        out_shape=(
            pltpu.VMEM(outer.shape, jnp.float32),
            pltpu.VMEM(outer.shape, jnp.float32),
            pltpu.VMEM((1, rows * lax.axis_size("fsdp"), width), jnp.bfloat16),
        ),
        in_specs=[anywhere, anywhere, anywhere, pl.BlockSpec(memory_space=pltpu.SMEM)],
        out_specs=(pl.BlockSpec(memory_space=pltpu.VMEM),) * 3,
        scratch_shapes=[
            full, full, full,
            wire(units, GROUP), wire(units, 2 * GROUP), wire(2 * GROUP), wire(units, GROUP), wire(units, GROUP),
            scales(GROUP), scales(GROUP), scales(2 * GROUP), scales(GROUP), scales(GROUP),
            sems(3, PARTS), sems(3), sems(3),
            sems(units), sems(units), sems(units), sems(units), sems(units), sems(units),
            sems(units, 7), sems(units, 7),
        ],
        compiler_params=pltpu.CompilerParams(
            collective_id=0, has_side_effects=True, vmem_limit_bytes=36 * 2**20
        ),
        name="outer_step",
    )(hbm(outer), hbm(inner), hbm(momentum), partner)
    vmem = lambda x: pltpu.with_memory_space_constraint(x, pltpu.VMEM)
    return pl.pallas_call(
        flush,
        out_shape=tuple(jax.ShapeDtypeStruct(x.shape, x.dtype) for x in results),
        in_specs=[anywhere] * 3,
        out_specs=(anywhere,) * 3,
        scratch_shapes=[sems(3)],
        compiler_params=pltpu.CompilerParams(vmem_limit_bytes=2 * 2**20),
        name="flush",
    )(*(vmem(x) for x in results))


def solution(mesh):
    return jax.shard_map(
        local,
        mesh=mesh,
        in_specs=(P("cuts", "fsdp", None), P("cuts", "fsdp", None), P("cuts", "fsdp", None), P()),
        out_specs=(P("cuts", "fsdp", None), P("cuts", "fsdp", None), P("cuts", None, None)),
        check_vma=False,
    )
```

```python
import functools

import jax
import jax.numpy as jnp
from jax import lax
from jax.experimental import pallas as pl
from jax.experimental.pallas import tpu as pltpu
from jax.sharding import PartitionSpec as P

momentum_decay = 0.6
outer_rate = 0.7
pull_weight = 0.5

MESH = pl.DeviceIdType.MESH
STEPS = 32767.0
GROUP = 8
LANES = 128
HEIGHT = 16
PARTS = 4
KINDS = ((0, 12), (2, 10), (4, 7), (6, 3), (8, 0))
LAGS = (-1, 2, 5, 8, 11, 14)


def terms(outer, inner, momentum):
    pull = (0.5 - 0.5 * pull_weight) * outer - 0.5 * inner
    half = 0.5 * momentum_decay * momentum
    return pull + half, (1.0 + momentum_decay) * pull + momentum_decay * half


def kernel(
    units, slices, slots, across_first, outer, inner, momentum, partner, new_outer, new_momentum, weights,
    o_v, i_v, m_v, packed, mixed, crossing, crossed, stage_out, stage, picked, final, inverse,
    scale, scale_mixed, scale_crossing, scale_crossed, scale_stage_out, scale_stage, scale_picked, scale_final,
    load_sem, scale_send, scale_recv, out1_send, out1_recv, half_send, half_recv, out2_send, out2_recv,
    gather_send, gather_recv,
):
    rows, width = o_v.shape
    levels, span = rows // HEIGHT, width // PARTS
    c, f = lax.axis_index("cuts"), lax.axis_index("fsdp")
    half, place = c // GROUP, c % GROUP
    base = half * GROUP
    y, xl = f // 2, f % 2

    def mate(k):
        return base + (place + k) % GROUP, f

    across = ((1 - half) * GROUP + place, f)
    beside = (c, y * 2 + 1 - xl)
    up = (c, ((y + 1) % 4) * 2 + xl)
    down = (c, ((y + 3) % 4) * 2 + xl)
    peers = [mate(k) for k in range(1, GROUP)] + [across, beside, up, down]

    def other(r):
        return (partner[r] // GROUP + r // GROUP) % 2

    def ranks(start):
        total, out = jnp.int32(0), []
        for k in range(GROUP):
            out.append(total)
            total = total + other(start + k)
        return out

    ours, theirs = ranks(base), ranks((1 - half) * GROUP)
    leave, source = [], []
    for n in range(slots):
        leave.append(sum(k * other(base + k) * (ours[k] == n).astype(jnp.int32) for k in range(GROUP)))
    for k in range(GROUP):
        p = partner[base + k]
        far = sum(theirs[i] * (p % GROUP == i).astype(jnp.int32) for i in range(GROUP))
        source.append(jnp.where(other(base + k) == 1, GROUP + jnp.minimum(far, slots - 1), p % GROUP))

    barrier = pltpu.get_barrier_semaphore()
    for peer in peers:
        pl.semaphore_signal(barrier, inc=1, device_id=peer, device_id_type=MESH)
    loads = [
        [
            pltpu.make_async_copy(
                src.at[0, :, pl.ds(p * span, span)], dst.at[:, pl.ds(p * span, span)], load_sem.at[k, p]
            )
            for k, (src, dst) in enumerate(((outer, o_v), (inner, i_v), (momentum, m_v)))
        ]
        for p in range(PARTS)
    ]
    for part in loads:
        for copy in part:
            copy.start()

    def tile(p, j, q):
        return pl.ds(pl.multiple_of(p * span + (j * slices + q) * LANES, LANES), LANES)

    def measure_scales(p):
        for copy in loads[p]:
            copy.wait()

        def one(j, carry):
            for q in range(slices):
                cols = tile(p, j, q)
                for row, term in zip((q, slices + q), terms(o_v[:, cols], i_v[:, cols], m_v[:, cols])):
                    top = jnp.max(jnp.abs(term), axis=0, keepdims=True)
                    scale[p, j, row : row + 1, :] = top * (1.0 / STEPS)
                    inverse[p, j, row : row + 1, :] = jnp.where(top > 1e-30, STEPS / jnp.maximum(top, 1e-30), 0.0)
            return carry

        lax.fori_loop(0, GROUP, one, 0)

    def where(u):
        return u // levels, pl.ds(pl.multiple_of((u % levels) * HEIGHT, HEIGHT), HEIGHT)

    def pack(u):
        p, here = where(u)

        def one(j, carry):
            for q in range(slices):
                cols = tile(p, j, q)
                first, second = terms(o_v[here, cols], i_v[here, cols], m_v[here, cols])
                a = jnp.round(first * inverse[p, j, q : q + 1, :]).astype(jnp.int32)
                b = jnp.round(second * inverse[p, j, slices + q : slices + q + 1, :]).astype(jnp.int32)
                packed[u, j, q * HEIGHT : (q + 1) * HEIGHT, :] = (a << 16) | (b & 0xFFFF)
            return carry

        lax.fori_loop(0, GROUP, one, 0)

    def spread(source, target, slot, send, recv):
        keep = pltpu.make_async_copy(source.at[place], target.at[slot], recv)
        keep.start()
        for k in range(1, GROUP):
            j = (place + k) % GROUP
            pltpu.make_async_remote_copy(
                src_ref=source.at[j], dst_ref=target.at[slot], send_sem=send, recv_sem=recv,
                device_id=mate(k), device_id_type=MESH,
            ).start()

    def wait(ref, sem):
        pltpu.make_async_copy(ref, ref, sem).wait()

    def first_of_part(u, do):
        pl.when(u % levels == 0)(lambda: do(u // levels))

    def send_out(u):
        pack(u)
        first_of_part(u, lambda p: spread(scale.at[p], scale_mixed.at[p], place, scale_send.at[0, p], scale_recv.at[0, p]))
        spread(packed.at[u], mixed.at[u], place, out1_send.at[u], out1_recv.at[u])

    def cross(mine, hold, outgoing, incoming, send, recv):
        hold[...] = mine[...]
        for n in range(slots):
            outgoing[n] = hold[leave[n]]
        if slots:
            pltpu.make_async_remote_copy(
                src_ref=outgoing, dst_ref=incoming, send_sem=send, recv_sem=recv,
                device_id=across, device_id_type=MESH,
            ).start()

    def swap_halves(u):
        def scales(p):
            wait(scale_mixed.at[p], scale_recv.at[0, p])
            cross(
                scale_mixed.at[p], scale_stage_out, scale_crossing.at[p], scale_crossed.at[p],
                scale_send.at[1, p], scale_recv.at[1, p],
            )

        first_of_part(u, scales)
        wait(mixed.at[u], out1_recv.at[u])
        cross(mixed.at[u], stage_out, crossing.at[u], crossed.at[u], half_send.at[u], half_recv.at[u])

    def pick(mine, incoming, hold, out, recv):
        hold[pl.ds(0, GROUP)] = mine[...]
        if slots:
            wait(incoming, recv)
            hold[pl.ds(GROUP, slots)] = incoming[...]
        for k in range(GROUP):
            out[k] = hold[source[k]]

    def send_back(u):
        def scales(p):
            pick(scale_mixed.at[p], scale_crossed.at[p], scale_stage, scale_picked.at[p], scale_recv.at[1, p])
            spread(scale_picked.at[p], scale_final.at[p], place, scale_send.at[2, p], scale_recv.at[2, p])

        first_of_part(u, scales)
        pick(mixed.at[u], crossed.at[u], stage, picked.at[u], half_recv.at[u])
        spread(picked.at[u], final.at[u], place, out2_send.at[u], out2_recv.at[u])

    def block(device, u):
        p, _ = where(u)
        start = pl.multiple_of(device * rows + (u % levels) * HEIGHT, HEIGHT)
        return weights.at[0, pl.ds(start, HEIGHT), pl.ds(pl.multiple_of(p * span, span), span)]

    def hand(u, owner, target, slot):
        pltpu.make_async_remote_copy(
            src_ref=block(owner, u), dst_ref=block(owner, u),
            send_sem=gather_send.at[u, slot], recv_sem=gather_recv.at[u, slot],
            device_id=target, device_id_type=MESH,
        ).start()

    def update(u):
        p, here = where(u)
        first_of_part(u, lambda part: wait(scale_final.at[part], scale_recv.at[2, part]))
        wait(final.at[u], out2_recv.at[u])
        there = pl.ds(pl.multiple_of(f * rows + (u % levels) * HEIGHT, HEIGHT), HEIGHT)

        def one(j, carry):
            for q in range(slices):
                cols = tile(p, j, q)
                word = final[u, j, q * HEIGHT : (q + 1) * HEIGHT, :]
                first = (word >> 16).astype(jnp.float32) * scale_final[p, j, q : q + 1, :]
                second = ((word << 16) >> 16).astype(jnp.float32) * scale_final[p, j, slices + q : slices + q + 1, :]
                own = o_v[here, cols]
                push = (0.5 + 0.5 * pull_weight) * own - 0.5 * i_v[here, cols]
                momentum_part = (0.5 * momentum_decay) * m_v[here, cols]
                new_momentum[0, here, cols] = momentum_part + push + first
                step = (1.0 + momentum_decay) * push + momentum_decay * momentum_part + second
                result = own - outer_rate * step
                new_outer[0, here, cols] = result
                weights[0, there, cols] = result.astype(jnp.bfloat16)
            return carry

        lax.fori_loop(0, GROUP, one, 0)
        hand(u, f, beside, 0)
        hand(u, f, up, 1)
        hand(u, f, down, 3)

    def arrived(u, slot):
        wait(block(f, u), gather_recv.at[u, slot])

    def by_x(u):
        return (u * across_first) // units == ((u + 1) * across_first) // units

    side, below, above = y * 2 + 1 - xl, ((y + 3) % 4) * 2 + xl, ((y + 1) % 4) * 2 + xl
    opposite, beyond = ((y + 2) % 4) * 2 + xl, 1 - 2 * xl

    def pass_near(u):
        @pl.when(by_x(u))
        def _():
            arrived(u, 0)
            hand(u, side, up, 2)
            hand(u, side, down, 4)

        @pl.when(jnp.logical_not(by_x(u)))
        def _():
            arrived(u, 1)
            hand(u, below, beside, 2)
            pl.when(u % 2 == 0)(lambda: hand(u, below, up, 5))
            arrived(u, 3)
            hand(u, above, beside, 4)
            pl.when(u % 2 == 1)(lambda: hand(u, above, down, 5))

    def pass_far(u):
        @pl.when(by_x(u) & (u % 2 == 0))
        def _():
            arrived(u, 1)
            hand(u, below, up, 5)
            arrived(u, 2)
            hand(u, below + beyond, up, 6)

        @pl.when(by_x(u) & (u % 2 == 1))
        def _():
            arrived(u, 3)
            hand(u, above, down, 5)
            arrived(u, 4)
            hand(u, above + beyond, down, 6)

        @pl.when(jnp.logical_not(by_x(u)))
        def _():
            arrived(u, 5)
            hand(u, opposite, beside, 6)

    measure_scales(0)
    pl.semaphore_wait(barrier, len(peers))
    send_out(0)
    for p in range(1, PARTS):
        measure_scales(p)

    def turn(t, carry):
        for stage_of, lag in zip((send_out, swap_halves, send_back, update, pass_near, pass_far), LAGS):
            first = 1 if stage_of is send_out else 0
            pl.when((t - lag >= first) & (t - lag < units))(functools.partial(stage_of, t - lag))
        return carry

    lax.fori_loop(0, units + LAGS[-1], turn, 0)

    seven = pl.ds(0, GROUP - 1)

    def drain(u, carry):
        @pl.when(by_x(u) & (u % 2 == 0))
        def _():
            arrived(u, 3)
            arrived(u, 4)
            arrived(u, 5)

        @pl.when(by_x(u) & (u % 2 == 1))
        def _():
            arrived(u, 1)
            arrived(u, 2)
            arrived(u, 5)

        @pl.when(jnp.logical_not(by_x(u)))
        def _():
            arrived(u, 0)
            arrived(u, 2)
            arrived(u, 4)

        arrived(u, 6)
        for slot in range(7):
            wait(block(f, u), gather_send.at[u, slot])
        wait(packed.at[u, seven], out1_send.at[u])
        if slots:
            wait(crossing.at[u], half_send.at[u])
        wait(picked.at[u, seven], out2_send.at[u])
        return carry

    lax.fori_loop(0, units, drain, 0)
    for p in range(PARTS):
        wait(scale.at[p, seven], scale_send.at[0, p])
        if slots:
            wait(scale_crossing.at[p], scale_send.at[1, p])
        wait(scale_picked.at[p, seven], scale_send.at[2, p])


def flush(*refs):
    count = len(refs) // 2
    copies = [pltpu.make_async_copy(refs[k], refs[count + k], refs[-1].at[k]) for k in range(count)]
    for copy in copies:
        copy.start()
    for copy in copies:
        copy.wait()


def local(outer, inner, momentum, partner):
    _, rows, width = outer.shape
    units = rows // HEIGHT * PARTS
    slices = width // (PARTS * GROUP * LANES)
    anywhere = pl.BlockSpec(memory_space=pl.ANY)
    wire = lambda *lead: pltpu.VMEM(lead + (slices * HEIGHT, LANES), jnp.int32)
    scales = lambda *lead: pltpu.VMEM(lead + (2 * slices, LANES), jnp.float32)
    sems = lambda *shape: pltpu.SemaphoreType.DMA(shape)
    full = pltpu.VMEM((rows, width), jnp.float32)
    hbm = lambda x: pltpu.with_memory_space_constraint(x, pltpu.HBM)

    def step(slots, across_first):
        room = max(slots, 1)
        return pl.pallas_call(
            functools.partial(kernel, units, slices, slots, across_first),
            out_shape=(
                pltpu.VMEM(outer.shape, jnp.float32),
                pltpu.VMEM(outer.shape, jnp.float32),
                pltpu.VMEM((1, rows * lax.axis_size("fsdp"), width), jnp.bfloat16),
            ),
            in_specs=[anywhere, anywhere, anywhere, pl.BlockSpec(memory_space=pltpu.SMEM)],
            out_specs=(pl.BlockSpec(memory_space=pltpu.VMEM),) * 3,
            scratch_shapes=[
                full, full, full,
                wire(units, GROUP), wire(units, GROUP), wire(units, room), wire(units, room), wire(GROUP), wire(GROUP + slots),
                wire(units, GROUP), wire(units, GROUP), scales(PARTS, GROUP),
                scales(PARTS, GROUP), scales(PARTS, GROUP), scales(PARTS, room), scales(PARTS, room),
                scales(GROUP), scales(GROUP + slots),
                scales(PARTS, GROUP), scales(PARTS, GROUP),
                sems(3, PARTS), sems(3, PARTS), sems(3, PARTS),
                sems(units), sems(units), sems(units), sems(units), sems(units), sems(units),
                sems(units, 7), sems(units, 7),
            ],
            compiler_params=pltpu.CompilerParams(
                collective_id=slots // 2, has_side_effects=True, vmem_limit_bytes=36 * 2**20
            ),
            name="outer_step",
        )

    def whole(slots, across_first):
        vmem = lambda x: pltpu.with_memory_space_constraint(x, pltpu.VMEM)

        def run(outer, inner, momentum, partner):
            results = step(slots, across_first)(hbm(outer), hbm(inner), hbm(momentum), partner)
            return pl.pallas_call(
                flush,
                out_shape=tuple(jax.ShapeDtypeStruct(x.shape, x.dtype) for x in results),
                in_specs=[anywhere] * 3,
                out_specs=(anywhere,) * 3,
                scratch_shapes=[sems(3)],
                compiler_params=pltpu.CompilerParams(vmem_limit_bytes=2 * 2**20),
                name="flush",
            )(*(vmem(x) for x in results))

        return run

    crossings = jnp.sum((partner[:GROUP] >= GROUP).astype(jnp.int32))
    return lax.switch(crossings >> 1, [whole(*kind) for kind in KINDS], outer, inner, momentum, partner)


def solution(mesh):
    return jax.shard_map(
        local,
        mesh=mesh,
        in_specs=(P("cuts", "fsdp", None), P("cuts", "fsdp", None), P("cuts", "fsdp", None), P()),
        out_specs=(P("cuts", "fsdp", None), P("cuts", "fsdp", None), P("cuts", None, None)),
        check_vma=False,
    )
```

```python
import functools

import jax
import jax.numpy as jnp
from jax import lax
from jax.experimental import pallas as pl
from jax.experimental.pallas import tpu as pltpu
from jax.sharding import PartitionSpec as P

momentum_decay = 0.6
outer_rate = 0.7
pull_weight = 0.5

MESH = pl.DeviceIdType.MESH
STEPS = 32767.0
GROUP = 8
LANES = 128
HEIGHT = 16
PARTS = 4
KINDS = ((0, 10, 4), (2, 8, 4), (4, 6, 4), (6, 3, 4), (8, 0, 4))
LAGS = (-1, 2, 5, 8, 11, 14)


def terms(outer, inner, momentum):
    pull = (0.5 - 0.5 * pull_weight) * outer - 0.5 * inner
    half = 0.5 * momentum_decay * momentum
    return pull + half, (1.0 + momentum_decay) * pull + momentum_decay * half


def kernel(
    units, slices, slots, y_early, y_late, outer, inner, momentum, partner, new_outer, new_momentum, weights,
    o_v, i_v, m_v, packed, mixed, crossing, crossed, stage_out, stage, picked, final, inverse,
    scale, scale_mixed, scale_crossing, scale_crossed, scale_stage_out, scale_stage, scale_picked, scale_final,
    load_sem, scale_send, scale_recv, out1_send, out1_recv, half_send, half_recv, out2_send, out2_recv,
    gather_send, gather_recv,
):
    rows, width = o_v.shape
    levels, span = rows // HEIGHT, width // PARTS
    c, f = lax.axis_index("cuts"), lax.axis_index("fsdp")
    half, place = c // GROUP, c % GROUP
    base = half * GROUP
    y, xl = f // 2, f % 2

    def mate(k):
        return base + (place + k) % GROUP, f

    across = ((1 - half) * GROUP + place, f)
    beside = (c, y * 2 + 1 - xl)
    up = (c, ((y + 1) % 4) * 2 + xl)
    down = (c, ((y + 3) % 4) * 2 + xl)
    peers = [mate(k) for k in range(1, GROUP)] + [across, beside, up, down]

    barrier = pltpu.get_barrier_semaphore()
    for peer in peers:
        pl.semaphore_signal(barrier, inc=1, device_id=peer, device_id_type=MESH)
    loads = [
        [
            pltpu.make_async_copy(
                src.at[0, :, pl.ds(p * span, span)], dst.at[:, pl.ds(p * span, span)], load_sem.at[k, p]
            )
            for k, (src, dst) in enumerate(((outer, o_v), (inner, i_v), (momentum, m_v)))
        ]
        for p in range(PARTS)
    ]
    for part in loads:
        for copy in part:
            copy.start()

    def other(r):
        return (partner[r] // GROUP + r // GROUP) % 2

    def ranks(start):
        total, out = jnp.int32(0), []
        for k in range(GROUP):
            out.append(total)
            total = total + other(start + k)
        return out

    ours, theirs = ranks(base), ranks((1 - half) * GROUP)
    leave, source = [], []
    for n in range(slots):
        leave.append(sum(k * other(base + k) * (ours[k] == n).astype(jnp.int32) for k in range(GROUP)))
    for k in range(GROUP):
        p = partner[base + k]
        far = sum(theirs[i] * (p % GROUP == i).astype(jnp.int32) for i in range(GROUP))
        source.append(jnp.where(other(base + k) == 1, GROUP + jnp.minimum(far, slots - 1), p % GROUP))

    def tile(p, j, q):
        return pl.ds(pl.multiple_of(p * span + (j * slices + q) * LANES, LANES), LANES)

    def wait(ref, sem):
        pltpu.make_async_copy(ref, ref, sem).wait()

    def measure_scales(p):
        cols = pl.ds(pl.multiple_of(p * span, span), span)
        for k, ref in enumerate((o_v, i_v, m_v)):
            wait(ref.at[:, cols], load_sem.at[k, p])

        def one(j, carry):
            for q in range(slices):
                cols = tile(p, j, q)
                for row, term in zip((q, slices + q), terms(o_v[:, cols], i_v[:, cols], m_v[:, cols])):
                    top = jnp.max(jnp.abs(term), axis=0, keepdims=True)
                    scale[p, j, row : row + 1, :] = top * (1.0 / STEPS)
                    inverse[p, j, row : row + 1, :] = jnp.where(top > 1e-30, STEPS / jnp.maximum(top, 1e-30), 0.0)
            return carry

        lax.fori_loop(0, GROUP, one, 0)

    def where(u):
        return u // levels, pl.ds(pl.multiple_of((u % levels) * HEIGHT, HEIGHT), HEIGHT)

    def pack(u):
        p, here = where(u)

        def one(j, carry):
            for q in range(slices):
                cols = tile(p, j, q)
                first, second = terms(o_v[here, cols], i_v[here, cols], m_v[here, cols])
                a = jnp.round(first * inverse[p, j, q : q + 1, :]).astype(jnp.int32)
                b = jnp.round(second * inverse[p, j, slices + q : slices + q + 1, :]).astype(jnp.int32)
                packed[u, j, q * HEIGHT : (q + 1) * HEIGHT, :] = (a << 16) | (b & 0xFFFF)
            return carry

        lax.fori_loop(0, GROUP, one, 0)

    def spread(source, target, slot, send, recv):
        keep = pltpu.make_async_copy(source.at[place], target.at[slot], recv)
        keep.start()
        for k in range(1, GROUP):
            j = (place + k) % GROUP
            pltpu.make_async_remote_copy(
                src_ref=source.at[j], dst_ref=target.at[slot], send_sem=send, recv_sem=recv,
                device_id=mate(k), device_id_type=MESH,
            ).start()

    def first_of_part(u, do):
        pl.when(u % levels == 0)(lambda: do(u // levels))

    def send_out(u):
        first_of_part(u, measure_scales)
        pack(u)
        spread_out(u)

    def spread_out(u):
        first_of_part(u, lambda p: spread(scale.at[p], scale_mixed.at[p], place, scale_send.at[0, p], scale_recv.at[0, p]))
        spread(packed.at[u], mixed.at[u], place, out1_send.at[u], out1_recv.at[u])

    def cross(mine, hold, outgoing, incoming, send, recv):
        hold[...] = mine[...]
        for n in range(slots):
            outgoing[n] = hold[leave[n]]
        if slots:
            pltpu.make_async_remote_copy(
                src_ref=outgoing, dst_ref=incoming, send_sem=send, recv_sem=recv,
                device_id=across, device_id_type=MESH,
            ).start()

    def swap_halves(u):
        def scales(p):
            wait(scale_mixed.at[p], scale_recv.at[0, p])
            cross(
                scale_mixed.at[p], scale_stage_out, scale_crossing.at[p], scale_crossed.at[p],
                scale_send.at[1, p], scale_recv.at[1, p],
            )

        first_of_part(u, scales)
        wait(mixed.at[u], out1_recv.at[u])
        cross(mixed.at[u], stage_out, crossing.at[u], crossed.at[u], half_send.at[u], half_recv.at[u])

    def pick(mine, incoming, hold, out, recv):
        hold[pl.ds(0, GROUP)] = mine[...]
        if slots:
            wait(incoming, recv)
            hold[pl.ds(GROUP, slots)] = incoming[...]
        for k in range(GROUP):
            out[k] = hold[source[k]]

    def send_back(u):
        def scales(p):
            pick(scale_mixed.at[p], scale_crossed.at[p], scale_stage, scale_picked.at[p], scale_recv.at[1, p])
            spread(scale_picked.at[p], scale_final.at[p], place, scale_send.at[2, p], scale_recv.at[2, p])

        first_of_part(u, scales)
        pick(mixed.at[u], crossed.at[u], stage, picked.at[u], half_recv.at[u])
        spread(picked.at[u], final.at[u], place, out2_send.at[u], out2_recv.at[u])

    def block(device, u):
        p, _ = where(u)
        start = pl.multiple_of(device * rows + (u % levels) * HEIGHT, HEIGHT)
        return weights.at[0, pl.ds(start, HEIGHT), pl.ds(pl.multiple_of(p * span, span), span)]

    def hand(u, owner, target, slot):
        pltpu.make_async_remote_copy(
            src_ref=block(owner, u), dst_ref=block(owner, u),
            send_sem=gather_send.at[u, slot], recv_sem=gather_recv.at[u, slot],
            device_id=target, device_id_type=MESH,
        ).start()

    def update(u):
        p, here = where(u)
        first_of_part(u, lambda part: wait(scale_final.at[part], scale_recv.at[2, part]))
        wait(final.at[u], out2_recv.at[u])
        there = pl.ds(pl.multiple_of(f * rows + (u % levels) * HEIGHT, HEIGHT), HEIGHT)

        def one(j, carry):
            for q in range(slices):
                cols = tile(p, j, q)
                word = final[u, j, q * HEIGHT : (q + 1) * HEIGHT, :]
                first = (word >> 16).astype(jnp.float32) * scale_final[p, j, q : q + 1, :]
                second = ((word << 16) >> 16).astype(jnp.float32) * scale_final[p, j, slices + q : slices + q + 1, :]
                own = o_v[here, cols]
                push = (0.5 + 0.5 * pull_weight) * own - 0.5 * i_v[here, cols]
                momentum_part = (0.5 * momentum_decay) * m_v[here, cols]
                new_momentum[0, here, cols] = momentum_part + push + first
                step = (1.0 + momentum_decay) * push + momentum_decay * momentum_part + second
                result = own - outer_rate * step
                new_outer[0, here, cols] = result
                weights[0, there, cols] = result.astype(jnp.bfloat16)
            return carry

        lax.fori_loop(0, GROUP, one, 0)
        hand(u, f, beside, 0)
        hand(u, f, up, 1)
        hand(u, f, down, 3)

    def arrived(u, slot):
        wait(block(f, u), gather_recv.at[u, slot])

    def y_first(u):
        late = units * 3 // 4
        return jnp.where(u < late, (u * y_early) // late, y_early + ((u - late) * y_late) // (units - late))

    def by_y(u):
        return y_first(u) != y_first(u + 1)

    def by_x(u):
        return y_first(u) == y_first(u + 1)

    def goes_up(u):
        return jnp.where(by_y(u), y_first(u), u - y_first(u)) % 2 == 0

    def goes_down(u):
        return jnp.logical_not(goes_up(u))

    side, below, above = y * 2 + 1 - xl, ((y + 3) % 4) * 2 + xl, ((y + 1) % 4) * 2 + xl
    opposite, beyond = ((y + 2) % 4) * 2 + xl, 1 - 2 * xl

    def pass_near(u):
        @pl.when(by_x(u))
        def _():
            arrived(u, 0)
            hand(u, side, up, 2)
            hand(u, side, down, 4)

        @pl.when(by_y(u))
        def _():
            arrived(u, 1)
            hand(u, below, beside, 2)
            pl.when(goes_up(u))(lambda: hand(u, below, up, 5))
            arrived(u, 3)
            hand(u, above, beside, 4)
            pl.when(goes_down(u))(lambda: hand(u, above, down, 5))

    def pass_far(u):
        @pl.when(by_x(u) & goes_up(u))
        def _():
            arrived(u, 1)
            hand(u, below, up, 5)
            arrived(u, 2)
            hand(u, below + beyond, up, 6)

        @pl.when(by_x(u) & goes_down(u))
        def _():
            arrived(u, 3)
            hand(u, above, down, 5)
            arrived(u, 4)
            hand(u, above + beyond, down, 6)

        @pl.when(by_y(u))
        def _():
            arrived(u, 5)
            hand(u, opposite, beside, 6)

    measure_scales(0)
    pack(0)
    pl.semaphore_wait(barrier, len(peers))
    spread_out(0)

    def turn(t, carry):
        for stage_of, lag in zip((send_out, swap_halves, send_back, update, pass_near, pass_far), LAGS):
            first = 1 if stage_of is send_out else 0
            pl.when((t - lag >= first) & (t - lag < units))(functools.partial(stage_of, t - lag))
        return carry

    lax.fori_loop(0, units + LAGS[-1], turn, 0)

    seven = pl.ds(0, GROUP - 1)

    def drain(u, carry):
        @pl.when(by_x(u) & goes_up(u))
        def _():
            arrived(u, 3)
            arrived(u, 4)
            arrived(u, 5)

        @pl.when(by_x(u) & goes_down(u))
        def _():
            arrived(u, 1)
            arrived(u, 2)
            arrived(u, 5)

        @pl.when(by_y(u))
        def _():
            arrived(u, 0)
            arrived(u, 2)
            arrived(u, 4)

        arrived(u, 6)
        for slot in range(7):
            wait(block(f, u), gather_send.at[u, slot])
        wait(packed.at[u, seven], out1_send.at[u])
        if slots:
            wait(crossing.at[u], half_send.at[u])
        wait(picked.at[u, seven], out2_send.at[u])
        return carry

    lax.fori_loop(0, units, drain, 0)
    for p in range(PARTS):
        wait(scale.at[p, seven], scale_send.at[0, p])
        if slots:
            wait(scale_crossing.at[p], scale_send.at[1, p])
        wait(scale_picked.at[p, seven], scale_send.at[2, p])


def flush(*refs):
    count = len(refs) // 2
    copies = [pltpu.make_async_copy(refs[k], refs[count + k], refs[-1].at[k]) for k in range(count)]
    for copy in copies:
        copy.start()
    for copy in copies:
        copy.wait()


def local(outer, inner, momentum, partner):
    _, rows, width = outer.shape
    units = rows // HEIGHT * PARTS
    slices = width // (PARTS * GROUP * LANES)
    anywhere = pl.BlockSpec(memory_space=pl.ANY)
    wire = lambda *lead: pltpu.VMEM(lead + (slices * HEIGHT, LANES), jnp.int32)
    scales = lambda *lead: pltpu.VMEM(lead + (2 * slices, LANES), jnp.float32)
    sems = lambda *shape: pltpu.SemaphoreType.DMA(shape)
    full = pltpu.VMEM((rows, width), jnp.float32)
    hbm = lambda x: pltpu.with_memory_space_constraint(x, pltpu.HBM)

    def step(slots, y_early, y_late):
        room = max(slots, 1)
        return pl.pallas_call(
            functools.partial(kernel, units, slices, slots, y_early, y_late),
            out_shape=(
                pltpu.VMEM(outer.shape, jnp.float32),
                pltpu.VMEM(outer.shape, jnp.float32),
                pltpu.VMEM((1, rows * lax.axis_size("fsdp"), width), jnp.bfloat16),
            ),
            in_specs=[anywhere, anywhere, anywhere, pl.BlockSpec(memory_space=pltpu.SMEM)],
            out_specs=(pl.BlockSpec(memory_space=pltpu.VMEM),) * 3,
            scratch_shapes=[
                full, full, full,
                wire(units, GROUP), wire(units, GROUP), wire(units, room), wire(units, room), wire(GROUP), wire(GROUP + slots),
                wire(units, GROUP), wire(units, GROUP), scales(PARTS, GROUP),
                scales(PARTS, GROUP), scales(PARTS, GROUP), scales(PARTS, room), scales(PARTS, room),
                scales(GROUP), scales(GROUP + slots),
                scales(PARTS, GROUP), scales(PARTS, GROUP),
                sems(3, PARTS), sems(3, PARTS), sems(3, PARTS),
                sems(units), sems(units), sems(units), sems(units), sems(units), sems(units),
                sems(units, 7), sems(units, 7),
            ],
            compiler_params=pltpu.CompilerParams(
                collective_id=slots // 2, has_side_effects=True, vmem_limit_bytes=36 * 2**20
            ),
            name="outer_step",
        )

    def whole(slots, y_early, y_late):
        vmem = lambda x: pltpu.with_memory_space_constraint(x, pltpu.VMEM)

        def run(outer, inner, momentum, partner):
            results = step(slots, y_early, y_late)(hbm(outer), hbm(inner), hbm(momentum), partner)
            return pl.pallas_call(
                flush,
                out_shape=tuple(jax.ShapeDtypeStruct(x.shape, x.dtype) for x in results),
                in_specs=[anywhere] * 3,
                out_specs=(anywhere,) * 3,
                scratch_shapes=[sems(3)],
                compiler_params=pltpu.CompilerParams(vmem_limit_bytes=2 * 2**20),
                name="flush",
            )(*(vmem(x) for x in results))

        return run

    crossings = jnp.sum((partner[:GROUP] >= GROUP).astype(jnp.int32))
    return lax.switch(crossings >> 1, [whole(*kind) for kind in KINDS], outer, inner, momentum, partner)


def solution(mesh):
    return jax.shard_map(
        local,
        mesh=mesh,
        in_specs=(P("cuts", "fsdp", None), P("cuts", "fsdp", None), P("cuts", "fsdp", None), P()),
        out_specs=(P("cuts", "fsdp", None), P("cuts", "fsdp", None), P("cuts", None, None)),
        check_vma=False,
    )
```

```python
import functools

import jax
import jax.numpy as jnp
from jax import lax
from jax.experimental import pallas as pl
from jax.experimental.pallas import tpu as pltpu
from jax.sharding import PartitionSpec as P

momentum_decay = 0.6
outer_rate = 0.7
pull_weight = 0.5

MESH = pl.DeviceIdType.MESH
STEPS = 32767.0
GROUP = 8
LANES = 128
HEIGHT = 16
PARTS = 4
KINDS = ((0, 10, 4), (2, 8, 4), (4, 6, 4), (6, 3, 4), (8, 1, 4))
FLUSHES = 4
LAGS = (-1, 3, 6, 9, 12, 15)


def terms(outer, inner, momentum):
    pull = (0.5 - 0.5 * pull_weight) * outer - 0.5 * inner
    half = 0.5 * momentum_decay * momentum
    return pull + half, (1.0 + momentum_decay) * pull + momentum_decay * half


def kernel(
    units, slices, slots, y_early, y_late, outer, inner, momentum, partner, new_outer, new_momentum, weights,
    o_v, i_v, m_v, packed, mixed, crossing, crossed, stage_out, stage, picked, final, inverse,
    scale, scale_mixed, scale_crossing, scale_crossed, scale_stage_out, scale_stage, scale_picked, scale_final,
    load_sem, scale_send, scale_recv, out1_send, out1_recv, half_send, half_recv, out2_send, out2_recv,
    gather_send, gather_recv,
):
    rows, width = o_v.shape
    levels, span = rows // HEIGHT, width // PARTS
    c, f = lax.axis_index("cuts"), lax.axis_index("fsdp")
    half, place = c // GROUP, c % GROUP
    base = half * GROUP
    y, xl = f // 2, f % 2

    mates = [(place + k) % GROUP for k in range(1, GROUP)]

    across = ((1 - half) * GROUP + place, f)
    beside = (c, y * 2 + 1 - xl)
    up = (c, ((y + 1) % 4) * 2 + xl)
    down = (c, ((y + 3) % 4) * 2 + xl)
    peers = [(base + j, f) for j in mates] + [across, beside, up, down]

    barrier = pltpu.get_barrier_semaphore()
    for peer in peers:
        pl.semaphore_signal(barrier, inc=1, device_id=peer, device_id_type=MESH)
    loads = [
        [
            pltpu.make_async_copy(
                src.at[0, :, pl.ds(p * span, span)], dst.at[:, pl.ds(p * span, span)], load_sem.at[k, p]
            )
            for k, (src, dst) in enumerate(((outer, o_v), (inner, i_v), (momentum, m_v)))
        ]
        for p in range(PARTS)
    ]
    for part in loads:
        for copy in part:
            copy.start()

    def other(r):
        return (partner[r] // GROUP + r // GROUP) % 2

    def ranks(start):
        total, out = jnp.int32(0), []
        for k in range(GROUP):
            out.append(total)
            total = total + other(start + k)
        return out

    ours, theirs = ranks(base), ranks((1 - half) * GROUP)
    leave, source = [], []
    for n in range(slots):
        leave.append(sum(k * other(base + k) * (ours[k] == n).astype(jnp.int32) for k in range(GROUP)))
    for k in range(GROUP):
        p = partner[base + k]
        far = sum(theirs[i] * (p % GROUP == i).astype(jnp.int32) for i in range(GROUP))
        source.append(jnp.where(other(base + k) == 1, GROUP + jnp.minimum(far, slots - 1), p % GROUP))

    def tile(p, j, q):
        return pl.ds(pl.multiple_of(p * span + (j * slices + q) * LANES, LANES), LANES)

    def wait(ref, sem):
        pltpu.make_async_copy(ref, ref, sem).wait()

    def measure_scales(p):
        cols = pl.ds(pl.multiple_of(p * span, span), span)
        for k, ref in enumerate((o_v, i_v, m_v)):
            wait(ref.at[:, cols], load_sem.at[k, p])

        def one(j, carry):
            for q in range(slices):
                cols = tile(p, j, q)
                for row, term in zip((q, slices + q), terms(o_v[:, cols], i_v[:, cols], m_v[:, cols])):
                    top = jnp.max(jnp.abs(term), axis=0, keepdims=True)
                    scale[p, j, row : row + 1, :] = top * (1.0 / STEPS)
                    inverse[p, j, row : row + 1, :] = jnp.where(top > 1e-30, STEPS / jnp.maximum(top, 1e-30), 0.0)
            return carry

        lax.fori_loop(0, GROUP, one, 0)

    def where(u):
        return lax.div(u, levels), pl.ds(pl.multiple_of(lax.rem(u, levels) * HEIGHT, HEIGHT), HEIGHT)

    def pack(u):
        p, here = where(u)

        def one(j, carry):
            for q in range(slices):
                cols = tile(p, j, q)
                first, second = terms(o_v[here, cols], i_v[here, cols], m_v[here, cols])
                a = jnp.round(first * inverse[p, j, q : q + 1, :]).astype(jnp.int32)
                b = jnp.round(second * inverse[p, j, slices + q : slices + q + 1, :]).astype(jnp.int32)
                packed[u, j, q * HEIGHT : (q + 1) * HEIGHT, :] = (a << 16) | (b & 0xFFFF)
            return carry

        lax.fori_loop(0, GROUP, one, 0)

    def spread(source, target, slot, send, recv):
        keep = pltpu.make_async_copy(source.at[place], target.at[slot], recv)
        keep.start()
        for j in mates:
            pltpu.make_async_remote_copy(
                src_ref=source.at[j], dst_ref=target.at[slot], send_sem=send, recv_sem=recv,
                device_id=(base + j, f), device_id_type=MESH,
            ).start()

    def first_of_part(u, do):
        pl.when(lax.rem(u, levels) == 0)(lambda: do(lax.div(u, levels)))

    def send_out(u):
        first_of_part(u, measure_scales)
        pack(u)
        spread_out(u)

    def spread_out(u):
        first_of_part(u, lambda p: spread(scale.at[p], scale_mixed.at[p], place, scale_send.at[0, p], scale_recv.at[0, p]))
        spread(packed.at[u], mixed.at[u], place, out1_send.at[u], out1_recv.at[u])

    def cross(mine, hold, outgoing, incoming, send, recv):
        hold[...] = mine[...]
        for n in range(slots):
            outgoing[n] = hold[leave[n]]
        if slots:
            pltpu.make_async_remote_copy(
                src_ref=outgoing, dst_ref=incoming, send_sem=send, recv_sem=recv,
                device_id=across, device_id_type=MESH,
            ).start()

    def swap_halves(u):
        def scales(p):
            wait(scale_mixed.at[p], scale_recv.at[0, p])
            cross(
                scale_mixed.at[p], scale_stage_out, scale_crossing.at[p], scale_crossed.at[p],
                scale_send.at[1, p], scale_recv.at[1, p],
            )

        first_of_part(u, scales)
        wait(mixed.at[u], out1_recv.at[u])
        cross(mixed.at[u], stage_out, crossing.at[u], crossed.at[u], half_send.at[u], half_recv.at[u])

    def pick(mine, incoming, hold, out, recv):
        hold[pl.ds(0, GROUP)] = mine[...]
        if slots:
            wait(incoming, recv)
            hold[pl.ds(GROUP, slots)] = incoming[...]
        for k in range(GROUP):
            out[k] = hold[source[k]]

    def send_back(u):
        def scales(p):
            pick(scale_mixed.at[p], scale_crossed.at[p], scale_stage, scale_picked.at[p], scale_recv.at[1, p])
            spread(scale_picked.at[p], scale_final.at[p], place, scale_send.at[2, p], scale_recv.at[2, p])

        first_of_part(u, scales)
        pick(mixed.at[u], crossed.at[u], stage, picked.at[u], half_recv.at[u])
        spread(picked.at[u], final.at[u], place, out2_send.at[u], out2_recv.at[u])

    def block(device, u):
        p, _ = where(u)
        start = pl.multiple_of(device * rows + lax.rem(u, levels) * HEIGHT, HEIGHT)
        return weights.at[0, pl.ds(start, HEIGHT), pl.ds(pl.multiple_of(p * span, span), span)]

    def hand(u, owner, target, slot):
        pltpu.make_async_remote_copy(
            src_ref=block(owner, u), dst_ref=block(owner, u),
            send_sem=gather_send.at[u, slot], recv_sem=gather_recv.at[u, slot],
            device_id=target, device_id_type=MESH,
        ).start()

    def update(u):
        p, here = where(u)
        first_of_part(u, lambda part: wait(scale_final.at[part], scale_recv.at[2, part]))
        wait(final.at[u], out2_recv.at[u])
        there = pl.ds(pl.multiple_of(f * rows + lax.rem(u, levels) * HEIGHT, HEIGHT), HEIGHT)

        def one(j, carry):
            for q in range(slices):
                cols = tile(p, j, q)
                word = final[u, j, q * HEIGHT : (q + 1) * HEIGHT, :]
                first = (word >> 16).astype(jnp.float32) * scale_final[p, j, q : q + 1, :]
                second = ((word << 16) >> 16).astype(jnp.float32) * scale_final[p, j, slices + q : slices + q + 1, :]
                own = o_v[here, cols]
                push = (0.5 + 0.5 * pull_weight) * own - 0.5 * i_v[here, cols]
                momentum_part = (0.5 * momentum_decay) * m_v[here, cols]
                new_momentum[0, here, cols] = momentum_part + push + first
                step = (1.0 + momentum_decay) * push + momentum_decay * momentum_part + second
                result = own - outer_rate * step
                new_outer[0, here, cols] = result
                weights[0, there, cols] = result.astype(jnp.bfloat16)
            return carry

        lax.fori_loop(0, GROUP, one, 0)
        hand(u, f, beside, 0)
        hand(u, f, up, 1)
        hand(u, f, down, 3)

    def arrived(u, slot):
        wait(block(f, u), gather_recv.at[u, slot])

    late = units * 3 // 4

    def y_first(u):
        return u * y_early // late if u < late else y_early + (u - late) * y_late // (units - late)

    firsts, ups = 0, 0
    for u in range(units):
        turned = y_first(u + 1) > y_first(u)
        firsts |= turned << u
        ups |= ((y_first(u) if turned else u - y_first(u)) % 2 == 0) << u

    def bit(mask, u):
        return (lax.shift_right_logical(jnp.int32(mask - ((mask >> 31) << 32)), u) & 1) == 1

    def by_y(u):
        return bit(firsts, u)

    def by_x(u):
        return jnp.logical_not(bit(firsts, u))

    def goes_up(u):
        return bit(ups, u)

    def goes_down(u):
        return jnp.logical_not(bit(ups, u))

    side, below, above = y * 2 + 1 - xl, ((y + 3) % 4) * 2 + xl, ((y + 1) % 4) * 2 + xl
    opposite, beyond = ((y + 2) % 4) * 2 + xl, 1 - 2 * xl

    def pass_near(u):
        @pl.when(by_x(u))
        def _():
            arrived(u, 0)
            hand(u, side, up, 2)
            hand(u, side, down, 4)

        @pl.when(by_y(u))
        def _():
            arrived(u, 1)
            hand(u, below, beside, 2)
            pl.when(goes_up(u))(lambda: hand(u, below, up, 5))
            arrived(u, 3)
            hand(u, above, beside, 4)
            pl.when(goes_down(u))(lambda: hand(u, above, down, 5))

    def pass_far(u):
        @pl.when(by_x(u) & goes_up(u))
        def _():
            arrived(u, 1)
            hand(u, below, up, 5)
            arrived(u, 2)
            hand(u, below + beyond, up, 6)

        @pl.when(by_x(u) & goes_down(u))
        def _():
            arrived(u, 3)
            hand(u, above, down, 5)
            arrived(u, 4)
            hand(u, above + beyond, down, 6)

        @pl.when(by_y(u))
        def _():
            arrived(u, 5)
            hand(u, opposite, beside, 6)

    measure_scales(0)
    pack(0)
    pl.semaphore_wait(barrier, len(peers))
    spread_out(0)

    def turn(t, carry):
        for stage_of, lag in zip((send_out, swap_halves, send_back, update, pass_near, pass_far), LAGS):
            first = 1 if stage_of is send_out else 0
            pl.when((t - lag >= first) & (t - lag < units))(functools.partial(stage_of, t - lag))
        return carry

    lax.fori_loop(0, units + LAGS[-1], turn, 0)

    seven = pl.ds(0, GROUP - 1)

    def drain(u, carry):
        @pl.when(by_x(u) & goes_up(u))
        def _():
            arrived(u, 3)
            arrived(u, 4)
            arrived(u, 5)

        @pl.when(by_x(u) & goes_down(u))
        def _():
            arrived(u, 1)
            arrived(u, 2)
            arrived(u, 5)

        @pl.when(by_y(u))
        def _():
            arrived(u, 0)
            arrived(u, 2)
            arrived(u, 4)

        arrived(u, 6)
        for slot in range(7):
            wait(block(f, u), gather_send.at[u, slot])
        wait(packed.at[u, seven], out1_send.at[u])
        if slots:
            wait(crossing.at[u], half_send.at[u])
        wait(picked.at[u, seven], out2_send.at[u])
        return carry

    lax.fori_loop(0, units, drain, 0)
    for p in range(PARTS):
        wait(scale.at[p, seven], scale_send.at[0, p])
        if slots:
            wait(scale_crossing.at[p], scale_send.at[1, p])
        wait(scale_picked.at[p, seven], scale_send.at[2, p])


def flush(*refs):
    count = len(refs) // 2
    copies = []
    for k in range(count):
        step = refs[k].shape[1] // FLUSHES
        for n in range(FLUSHES):
            piece = pl.ds(n * step, step)
            copies.append(pltpu.make_async_copy(refs[k].at[:, piece], refs[count + k].at[:, piece], refs[-1].at[k, n]))
    for copy in copies:
        copy.start()
    for copy in copies:
        copy.wait()


def local(outer, inner, momentum, partner):
    _, rows, width = outer.shape
    units = rows // HEIGHT * PARTS
    slices = width // (PARTS * GROUP * LANES)
    anywhere = pl.BlockSpec(memory_space=pl.ANY)
    wire = lambda *lead: pltpu.VMEM(lead + (slices * HEIGHT, LANES), jnp.int32)
    scales = lambda *lead: pltpu.VMEM(lead + (2 * slices, LANES), jnp.float32)
    sems = lambda *shape: pltpu.SemaphoreType.DMA(shape)
    full = pltpu.VMEM((rows, width), jnp.float32)
    hbm = lambda x: pltpu.with_memory_space_constraint(x, pltpu.HBM)

    def step(slots, y_early, y_late):
        room = max(slots, 1)
        return pl.pallas_call(
            functools.partial(kernel, units, slices, slots, y_early, y_late),
            out_shape=(
                pltpu.VMEM(outer.shape, jnp.float32),
                pltpu.VMEM(outer.shape, jnp.float32),
                pltpu.VMEM((1, rows * lax.axis_size("fsdp"), width), jnp.bfloat16),
            ),
            in_specs=[anywhere, anywhere, anywhere, pl.BlockSpec(memory_space=pltpu.SMEM)],
            out_specs=(pl.BlockSpec(memory_space=pltpu.VMEM),) * 3,
            scratch_shapes=[
                full, full, full,
                wire(units, GROUP), wire(units, GROUP), wire(units, room), wire(units, room), wire(GROUP), wire(GROUP + slots),
                wire(units, GROUP), wire(units, GROUP), scales(PARTS, GROUP),
                scales(PARTS, GROUP), scales(PARTS, GROUP), scales(PARTS, room), scales(PARTS, room),
                scales(GROUP), scales(GROUP + slots),
                scales(PARTS, GROUP), scales(PARTS, GROUP),
                sems(3, PARTS), sems(3, PARTS), sems(3, PARTS),
                sems(units), sems(units), sems(units), sems(units), sems(units), sems(units),
                sems(units, 7), sems(units, 7),
            ],
            compiler_params=pltpu.CompilerParams(
                collective_id=slots // 2, has_side_effects=True, vmem_limit_bytes=36 * 2**20
            ),
            name="outer_step",
        )

    def whole(slots, y_early, y_late):
        vmem = lambda x: pltpu.with_memory_space_constraint(x, pltpu.VMEM)

        def run(outer, inner, momentum, partner):
            results = step(slots, y_early, y_late)(hbm(outer), hbm(inner), hbm(momentum), partner)
            return pl.pallas_call(
                flush,
                out_shape=tuple(jax.ShapeDtypeStruct(x.shape, x.dtype) for x in results),
                in_specs=[anywhere] * 3,
                out_specs=(anywhere,) * 3,
                scratch_shapes=[sems(3, FLUSHES)],
                compiler_params=pltpu.CompilerParams(vmem_limit_bytes=2 * 2**20),
                name="flush",
            )(*(vmem(x) for x in results))

        return run

    crossings = jnp.sum((partner[:GROUP] >= GROUP).astype(jnp.int32))
    return lax.switch(crossings >> 1, [whole(*kind) for kind in KINDS], outer, inner, momentum, partner)


def solution(mesh):
    return jax.shard_map(
        local,
        mesh=mesh,
        in_specs=(P("cuts", "fsdp", None), P("cuts", "fsdp", None), P("cuts", "fsdp", None), P()),
        out_specs=(P("cuts", "fsdp", None), P("cuts", "fsdp", None), P("cuts", None, None)),
        check_vma=False,
    )
```
